32 devices in a mesh: aux: 2 (over core), pair: 16 (over z, y, x).
Axes of the slice: x: 2, y: 2, z: 4, core: 2. Of those that a mesh axis runs over, the one named last changes fastest.
Arguments:
- metric_factor: bfloat16 [16384, 16384], P('pair', 'aux'), as said below
- three_centre: bfloat16 [16384, 1536], P('aux', 'pair')
- occ_energy: float32 [2], replicated, may hold values from -2 to -0.3
- virt_energy: float32 [768], replicated, may hold values from 0.2 to 3
Outputs:
- amplitudes: float32 [1536, 1536], P('pair', 'aux')
- energy: float32 [], replicated
The draws below stay inside these ranges and needn't reach their ends.
Inputs may be any that keep to these rules, and one draw needn't show every extreme that they name: metric_factor is lower triangular: every entry above the diagonal is zero, and its diagonal lies between 0.5 and 1.5.
All inputs are finite; a program needn't handle non-finite values.
Results may differ from the reference program's by a relative error of at most 0.0023.
Values may be sent and summed in bfloat16 or wider, within the bound.
No kernel may reach another device: no remote copies, remote signals or barrier semaphores. Data moves between devices by JAX's collectives and lax.ppermute only.
A program may use at most 128 MiB of HBM per device.

```python
import math
import jax
import jax.numpy as jnp
from jax import lax

NAUX = 16384
NVIRT = 768
NOCC_B = 2
NP = 1536


def draw_metric_factor(key, part):
    first, second = jax.random.split(jax.random.fold_in(key, 11))
    row_index = lax.broadcasted_iota(jnp.int32, (NAUX, NAUX), 0)
    col_index = lax.broadcasted_iota(jnp.int32, (NAUX, NAUX), 1)
    below = jax.random.normal(first, (NAUX, NAUX), jnp.float32)
    below = below * (1.5 / math.sqrt(NAUX))
    diagonal = jax.random.uniform(second, (NAUX,), jnp.float32, 0.5, 1.5)
    result = jnp.where(row_index > col_index, below, 0.0)
    return (result + jnp.where(row_index == col_index, diagonal[None, :], 0.0)).astype(jnp.bfloat16)


def draw_three_centre(key, part):
    first, second = jax.random.split(jax.random.fold_in(key, 23), 2)
    column_scale = jnp.exp(jax.random.uniform(second, (NP,), jnp.float32, math.log(0.5), math.log(2.0)))
    base = jax.random.normal(first, (NAUX, NP), jnp.float32)
    return (base * column_scale[None, :] * (8.0 / math.sqrt(NAUX))).astype(jnp.bfloat16)


def setup_inputs(seed: int = 0) -> dict:
    splits = jax.random.split(jax.random.key(seed), 5)
    metric_factor = draw_metric_factor(jax.random.fold_in(splits[4], 71), 0)
    three_centre = draw_three_centre(jax.random.fold_in(splits[4], 71), 0)
    occ_energy = jnp.clip(jax.random.uniform(splits[2], (NOCC_B,), jnp.float32, -2.0, -0.3), -2.0, -0.3)
    virt_energy = jnp.clip(jax.random.uniform(splits[3], (NVIRT,), jnp.float32, 0.2, 3.0), 0.2, 3.0)
    return dict(metric_factor=metric_factor, three_centre=three_centre, occ_energy=occ_energy, virt_energy=virt_energy)


def reference(metric_factor, three_centre, occ_energy, virt_energy):
    band_rows = NAUX // 8
    pieces = []
    for block in range(8):
        lower = metric_factor[block * band_rows:(block + 1) * band_rows, :(block + 1) * band_rows]
        pieces.append(jnp.dot(lower, three_centre[:(block + 1) * band_rows], preferred_element_type=jnp.float32))
    fitted = jnp.concatenate(pieces, axis=0).astype(jnp.bfloat16)
    integrals = lax.dot_general(fitted, fitted, (((0,), (0,)), ((), ())), preferred_element_type=jnp.float32)
    pair_gap = (virt_energy[None, :] - occ_energy[:, None]).reshape(-1)
    denominator = pair_gap[:, None] + pair_gap[None, :]
    amplitudes = integrals / denominator
    energy = -jnp.sum(integrals * amplitudes)
    return amplitudes, energy
```

```python
import jax
import jax.numpy as jnp
from jax import lax
from jax.sharding import PartitionSpec as P


def total_of(value, axes):
    count = lax.axis_size(axes)
    sent = jnp.broadcast_to(value, (count, 8, 128))
    return jnp.sum(lax.all_to_all(sent, axes, 0, 0, tiled=True)[:, 0, 0])


def shards(metric_factor, three_centre, occ_energy, virt_energy):
    aux_count = lax.axis_size("aux")
    pair_count = lax.axis_size("pair")
    aux_id = lax.axis_index("aux")
    pair_id = lax.axis_index("pair")
    pairs_total = three_centre.shape[1] * pair_count
    share_cols = pairs_total // aux_count
    share_rows = pairs_total // pair_count
    partial_fit = jnp.dot(
        metric_factor,
        lax.all_gather(three_centre, "pair", axis=1, tiled=True),
        preferred_element_type=jnp.float32,
    )
    own_share = lax.psum_scatter(partial_fit, "aux", scatter_dimension=1, tiled=True).astype(
        jnp.bfloat16
    )
    fitted = lax.all_gather(own_share, "aux", axis=1, tiled=True)
    partial_tiles = lax.dot_general(
        fitted, own_share, (((0,), (0,)), ((), ())), preferred_element_type=jnp.float32
    ).astype(jnp.bfloat16)
    tiles = lax.all_to_all(partial_tiles, "pair", 0, 0, tiled=True)
    integrals = jnp.sum(
        tiles.reshape(pair_count, share_rows, share_cols).astype(jnp.float32), axis=0
    )
    pair_gap = (virt_energy[None, :] - occ_energy[:, None]).reshape(-1)
    row_gap = lax.dynamic_slice_in_dim(pair_gap, pair_id * share_rows, share_rows, 0)
    col_gap = lax.dynamic_slice_in_dim(pair_gap, aux_id * share_cols, share_cols, 0)
    denominator = row_gap[:, None] + col_gap[None, :]
    amplitudes = integrals / denominator
    energy = -total_of(jnp.sum(integrals * amplitudes), ("aux", "pair"))
    return (amplitudes, energy)


def solution(mesh):
    in_specs = (P("pair", "aux"), P("aux", "pair"), P(), P())
    out_specs = (P("pair", "aux"), P())
    return jax.shard_map(shards, mesh=mesh, in_specs=in_specs, out_specs=out_specs, check_vma=False)
```

```python
import functools

import jax
import jax.numpy as jnp
from jax import lax
from jax.experimental import pallas as pl
from jax.experimental.pallas import tpu as pltpu
from jax.sharding import PartitionSpec as P

AXES = ("aux", "pair")
LAYERS = 4
PLANE = 4
TURN = (1, 2)


def total_of(value, axes):
    count = lax.axis_size(axes)
    sent = jnp.broadcast_to(value, (count, 8, 128))
    return jnp.sum(lax.all_to_all(sent, axes, 0, 0, tiled=True)[:, 0, 0])


def nt_dot(left, right):
    return lax.dot_general(
        left, right, (((1,), (1,)), ((), ())), preferred_element_type=jnp.float32
    )


def outputs(tiles, occ_energy, virt_energy):
    pair_count, share_rows, share_cols = tiles.shape
    aux_id = lax.axis_index("aux")
    pair_id = lax.axis_index("pair")
    integrals = jnp.sum(tiles.astype(jnp.float32), axis=0)
    pair_gap = (virt_energy[None, :] - occ_energy[:, None]).reshape(-1)
    row_gap = lax.dynamic_slice_in_dim(pair_gap, pair_id * share_rows, share_rows, 0)
    col_gap = lax.dynamic_slice_in_dim(pair_gap, aux_id * share_cols, share_cols, 0)
    denominator = row_gap[:, None] + col_gap[None, :]
    amplitudes = integrals / denominator
    energy = -total_of(jnp.sum(integrals * amplitudes), AXES)
    return (amplitudes, energy)


def shards_any(metric_factor, three_centre, occ_energy, virt_energy):
    aux_count = lax.axis_size("aux")
    pair_count = lax.axis_size("pair")
    pairs_total = three_centre.shape[1] * pair_count
    share_cols = pairs_total // aux_count
    share_rows = pairs_total // pair_count
    partial_fit = jnp.dot(
        metric_factor,
        lax.all_gather(three_centre, "pair", axis=1, tiled=True),
        preferred_element_type=jnp.float32,
    )
    own_share = lax.psum_scatter(partial_fit, "aux", scatter_dimension=1, tiled=True).astype(
        jnp.bfloat16
    )
    fitted = lax.all_gather(own_share, "aux", axis=1, tiled=True)
    partial_tiles = lax.dot_general(
        fitted, own_share, (((0,), (0,)), ((), ())), preferred_element_type=jnp.float32
    ).astype(jnp.bfloat16)
    tiles = lax.all_to_all(partial_tiles, "pair", 0, 0, tiled=True)
    return outputs(tiles.reshape(pair_count, share_rows, share_cols), occ_energy, virt_energy)


def layers_of(core):
    return range(0, LAYERS) if core == 0 else range(LAYERS // 2, LAYERS)


def along(turn):
    pairs = []
    for core in range(2):
        for z in layers_of(core):
            at = (core * LAYERS + z) * PLANE
            pairs += [(at + i, at + (i ^ turn[core])) for i in range(PLANE)]
    return pairs


def climbs(stage):
    steps = [[(z, (z + 1) % LAYERS) for z in range(LAYERS)]]
    steps.append([(z, z + 1) for z in range(stage - 1, LAYERS - 1)])
    if stage == LAYERS - 1:
        steps[1].append((LAYERS - 1, LAYERS - 2))
    pairs = []
    for core in range(2):
        for source, target in steps[core]:
            at, to = [(core * LAYERS + z) * PLANE for z in (source, target)]
            pairs += [(at + i, to + i) for i in range(PLANE)]
    return pairs


def tied(value, after):
    return lax.optimization_barrier((value, *after))[0] if after else value


def fit_kernel(flags, own, near, far, factor, out):
    wide = own.shape[0]

    @pl.when(flags[0] == 1)
    def _():
        total = lax.dot_general(
            jnp.concatenate([own[...], near[...], far[...]]),
            factor[...],
            (((1,), (1,)), ((), ())),
            preferred_element_type=jnp.float32,
        ).astype(out.dtype)
        turned = flags[1] * wide
        places = [
            0,
            pl.multiple_of(2 * wide - turned, 32),
            pl.multiple_of(wide + turned, 32),
            3 * wide,
        ]
        for i, at in enumerate(places):
            out[pl.ds(at, wide), :] = total[i * wide : (i + 1) * wide]

    @pl.when(flags[0] == 0)
    def _():
        out[...] = jnp.zeros(out.shape, out.dtype)


def fit(flags, pieces, factor):
    depth = factor.shape[1]
    wide = sum(piece.shape[0] for piece in pieces)
    rows = factor.shape[0]
    step = min(rows, 256)
    return pl.pallas_call(
        fit_kernel,
        out_shape=jax.ShapeDtypeStruct((wide, rows), jnp.bfloat16),
        grid_spec=pltpu.PrefetchScalarGridSpec(
            num_scalar_prefetch=1,
            grid=(rows // step,),
            in_specs=[pl.BlockSpec(piece.shape, lambda i, flags: (0, 0)) for piece in pieces]
            + [pl.BlockSpec((step, depth), lambda i, flags: (i * flags[0], 0))],
            out_specs=pl.BlockSpec((wide, step), lambda i, flags: (0, i)),
        ),
        compiler_params=pltpu.CompilerParams(vmem_limit_bytes=40 << 20),
        cost_estimate=pl.CostEstimate(
            flops=2 * wide * depth * rows,
            bytes_accessed=2 * (depth * (wide + rows) + wide * rows),
            transcendentals=0,
        ),
    )(flags, *pieces, factor)


def shards_stacked(metric_factor, three_centre, occ_energy, virt_energy):
    aux_id = lax.axis_index("aux")
    pair_id = lax.axis_index("pair")
    layer = pair_id // PLANE
    place = pair_id % PLANE
    share_rows = three_centre.shape[1]
    pair_count = LAYERS * PLANE
    pairs_total = share_rows * pair_count
    share_cols = pairs_total // 2
    rows = metric_factor.shape[0]
    own = three_centre.T
    needed = jnp.logical_or(aux_id == 0, layer >= LAYERS // 2)
    crossed = []

    def cross(piece, turn, after):
        after = [*crossed[-2:][: max(len(crossed) - 1, 0)][:1], *after]
        crossed.append(lax.ppermute(tied(piece, after), AXES, along(turn)))
        return crossed[-1]

    def first(piece, after=()):
        return [piece, cross(piece, TURN, after)]

    def second(held, after=()):
        return [*held, cross(jnp.concatenate(held), TURN[::-1], after)]

    def climb(piece, stage, after=()):
        return lax.ppermute(tied(piece, after), AXES, climbs(stage))

    flags = jnp.stack([needed, aux_id == 0]).astype(jnp.int32)

    def fitted_of(pieces):
        partial = fit(flags, pieces, metric_factor)
        other = lax.ppermute(partial, "aux", [(0, 1), (1, 0)])
        total = partial.astype(jnp.float32) + other.astype(jnp.float32)
        return partial, total.astype(jnp.bfloat16)

    above_1 = climb(own, 1)
    held_0 = first(own)
    plane_0 = second(held_0)
    held_1 = first(above_1)
    above_2 = climb(above_1, 2, held_0[1:])
    plane_1 = second(held_1)
    held_2 = first(above_2)
    turning = jnp.logical_and(aux_id == 1, layer == LAYERS - 1)
    above_3 = climb(jnp.where(turning, own, above_2), 3, held_1[1:])
    plane_2 = second(held_2)
    partial_0, fitted_0 = fitted_of(plane_0)
    held_3 = first(above_3, [partial_0])
    partial_1, fitted_1 = fitted_of(plane_1)
    plane_3 = second(held_3, [partial_1])
    partial_2, fitted_2 = fitted_of(plane_2)
    plane_3[2] = tied(plane_3[2], [partial_2])
    fitted = jnp.concatenate([fitted_0, fitted_1, fitted_2, fitted_of(plane_3)[1]])
    blocks = fitted.reshape(pair_count, share_rows, rows)
    ordered = []
    for z in range(LAYERS):
        slot = (layer - z) % LAYERS
        for where in range(PLANE):
            offset = place ^ where
            at = slot * PLANE + offset
            ordered.append(lax.dynamic_index_in_dim(blocks, at, 0, keepdims=False))
    fitted = jnp.concatenate(ordered)
    own_share = lax.dynamic_slice_in_dim(fitted, aux_id * share_cols, share_cols, 0)
    partial_tiles = nt_dot(fitted, own_share).astype(jnp.bfloat16)
    tiles = lax.all_to_all(
        partial_tiles.reshape(pair_count, share_rows, share_cols), "pair", 0, 0, tiled=True
    )
    return outputs(tiles, occ_energy, virt_energy)


def solution(mesh):
    in_specs = (P("pair", "aux"), P("aux", "pair"), P(), P())
    out_specs = (P("pair", "aux"), P())
    stacked = mesh.shape["aux"] == 2 and mesh.shape["pair"] == LAYERS * PLANE
    return jax.shard_map(
        shards_stacked if stacked else shards_any,
        mesh=mesh,
        in_specs=in_specs,
        out_specs=out_specs,
        check_vma=False,
    )
```

```python
import functools

import jax
import jax.numpy as jnp
from jax import lax
from jax.experimental import pallas as pl
from jax.experimental.pallas import tpu as pltpu
from jax.sharding import PartitionSpec as P

AXES = ("aux", "pair")
LAYERS = 4
PLANE = 4
TURN = (1, 2)


def total_of(value, axes):
    count = lax.axis_size(axes)
    sent = jnp.broadcast_to(value, (count, 8, 128))
    return jnp.sum(lax.all_to_all(sent, axes, 0, 0, tiled=True)[:, 0, 0])


def nt_dot(left, right):
    return lax.dot_general(
        left, right, (((1,), (1,)), ((), ())), preferred_element_type=jnp.float32
    )


def outputs(tiles, occ_energy, virt_energy):
    pair_count, share_rows, share_cols = tiles.shape
    aux_id = lax.axis_index("aux")
    pair_id = lax.axis_index("pair")
    integrals = jnp.sum(tiles.astype(jnp.float32), axis=0)
    pair_gap = (virt_energy[None, :] - occ_energy[:, None]).reshape(-1)
    row_gap = lax.dynamic_slice_in_dim(pair_gap, pair_id * share_rows, share_rows, 0)
    col_gap = lax.dynamic_slice_in_dim(pair_gap, aux_id * share_cols, share_cols, 0)
    denominator = row_gap[:, None] + col_gap[None, :]
    amplitudes = integrals / denominator
    energy = -total_of(jnp.sum(integrals * amplitudes), AXES)
    return (amplitudes, energy)


def shards_any(metric_factor, three_centre, occ_energy, virt_energy):
    aux_count = lax.axis_size("aux")
    pair_count = lax.axis_size("pair")
    pairs_total = three_centre.shape[1] * pair_count
    share_cols = pairs_total // aux_count
    share_rows = pairs_total // pair_count
    partial_fit = jnp.dot(
        metric_factor,
        lax.all_gather(three_centre, "pair", axis=1, tiled=True),
        preferred_element_type=jnp.float32,
    )
    own_share = lax.psum_scatter(partial_fit, "aux", scatter_dimension=1, tiled=True).astype(
        jnp.bfloat16
    )
    fitted = lax.all_gather(own_share, "aux", axis=1, tiled=True)
    partial_tiles = lax.dot_general(
        fitted, own_share, (((0,), (0,)), ((), ())), preferred_element_type=jnp.float32
    ).astype(jnp.bfloat16)
    tiles = lax.all_to_all(partial_tiles, "pair", 0, 0, tiled=True)
    return outputs(tiles.reshape(pair_count, share_rows, share_cols), occ_energy, virt_energy)


def layers_of(core):
    return range(0, LAYERS) if core == 0 else range(LAYERS // 2, LAYERS)


def along(turn):
    pairs = []
    for core in range(2):
        for z in layers_of(core):
            at = (core * LAYERS + z) * PLANE
            pairs += [(at + i, at + (i ^ turn[core])) for i in range(PLANE)]
    return pairs


def climbs(stage):
    steps = [[(z, (z + 1) % LAYERS) for z in range(LAYERS)]]
    steps.append([(z, z + 1) for z in range(stage - 1, LAYERS - 1)])
    if stage == LAYERS - 1:
        steps[1].append((LAYERS - 1, LAYERS - 2))
    pairs = []
    for core in range(2):
        for source, target in steps[core]:
            at, to = [(core * LAYERS + z) * PLANE for z in (source, target)]
            pairs += [(at + i, to + i) for i in range(PLANE)]
    return pairs


def tied(value, after):
    return lax.optimization_barrier((value, *after))[0] if after else value


def fit_kernel(flags, own, near, far, both, factor, out):
    wide = own.shape[0]

    @pl.when(flags[0] == 1)
    def _():
        total = lax.dot_general(
            jnp.concatenate([own[...], near[...], far[...], both[...]]),
            factor[...],
            (((1,), (1,)), ((), ())),
            preferred_element_type=jnp.float32,
        ).astype(out.dtype)
        turned = flags[1] * wide
        places = [
            0,
            pl.multiple_of(2 * wide - turned, 32),
            pl.multiple_of(wide + turned, 32),
            3 * wide,
        ]
        for i, at in enumerate(places):
            out[pl.ds(at, wide), :] = total[i * wide : (i + 1) * wide]

    @pl.when(flags[0] == 0)
    def _():
        out[...] = jnp.zeros(out.shape, out.dtype)


def fit(flags, pieces, factor):
    depth = factor.shape[1]
    wide = sum(piece.shape[0] for piece in pieces)
    rows = factor.shape[0]
    step = min(rows, 256)
    return pl.pallas_call(
        fit_kernel,
        out_shape=jax.ShapeDtypeStruct((wide, rows), jnp.bfloat16),
        grid_spec=pltpu.PrefetchScalarGridSpec(
            num_scalar_prefetch=1,
            grid=(rows // step,),
            in_specs=[pl.BlockSpec(piece.shape, lambda i, flags: (0, 0)) for piece in pieces]
            + [pl.BlockSpec((step, depth), lambda i, flags: (i * flags[0], 0))],
            out_specs=pl.BlockSpec((wide, step), lambda i, flags: (0, i)),
        ),
        compiler_params=pltpu.CompilerParams(vmem_limit_bytes=40 << 20),
        cost_estimate=pl.CostEstimate(
            flops=2 * wide * depth * rows,
            bytes_accessed=2 * (depth * (wide + rows) + wide * rows),
            transcendentals=0,
        ),
    )(flags, *pieces, factor)


def shards_stacked(metric_factor, three_centre, occ_energy, virt_energy):
    aux_id = lax.axis_index("aux")
    pair_id = lax.axis_index("pair")
    layer = pair_id // PLANE
    place = pair_id % PLANE
    share_rows = three_centre.shape[1]
    pair_count = LAYERS * PLANE
    pairs_total = share_rows * pair_count
    share_cols = pairs_total // 2
    rows = metric_factor.shape[0]
    own = three_centre.T
    needed = jnp.logical_or(aux_id == 0, layer >= LAYERS // 2)
    crossed = []

    def cross(piece, turn, after=()):
        after = [*crossed[-4:][: max(len(crossed) - 3, 0)][:1], *after]
        crossed.append(lax.ppermute(tied(piece, after), AXES, along(turn)))
        return crossed[-1]

    def spread(piece, after=(), near=None):
        near = cross(piece, TURN) if near is None else near
        far = cross(piece, TURN[::-1])
        return [piece, near, far, cross(near, TURN[::-1], after)]

    def climb(piece, stage, after=()):
        return lax.ppermute(tied(piece, after), AXES, climbs(stage))

    flags = jnp.stack([needed, aux_id == 0]).astype(jnp.int32)

    def fitted_of(pieces):
        partial = fit(flags, pieces, metric_factor)
        other = lax.ppermute(partial, "aux", [(0, 1), (1, 0)])
        total = partial.astype(jnp.float32) + other.astype(jnp.float32)
        return partial, total.astype(jnp.bfloat16)

    above_1 = climb(own, 1)
    plane_0 = spread(own)
    above_2 = climb(above_1, 2, plane_0[1:2])
    plane_1 = spread(above_1)
    turning = jnp.logical_and(aux_id == 1, layer == LAYERS - 1)
    above_3 = climb(jnp.where(turning, own, above_2), 3, plane_1[1:2])
    partial_0, fitted_0 = fitted_of(plane_0)
    plane_2 = spread(above_2)
    partial_1, fitted_1 = fitted_of(plane_1)
    near_3 = climb(jnp.where(turning, plane_0[1], plane_2[1]), 3)
    plane_3 = spread(above_3, [], near_3)
    partial_2, fitted_2 = fitted_of(plane_2)
    plane_3[3] = tied(plane_3[3], [partial_2])
    fitted = jnp.concatenate([fitted_0, fitted_1, fitted_2, fitted_of(plane_3)[1]])
    blocks = fitted.reshape(pair_count, share_rows, rows)
    ordered = []
    for z in range(LAYERS):
        slot = (layer - z) % LAYERS
        for where in range(PLANE):
            offset = place ^ where
            at = slot * PLANE + offset
            ordered.append(lax.dynamic_index_in_dim(blocks, at, 0, keepdims=False))
    fitted = jnp.concatenate(ordered)
    own_share = lax.dynamic_slice_in_dim(fitted, aux_id * share_cols, share_cols, 0)
    partial_tiles = nt_dot(fitted, own_share).astype(jnp.bfloat16)
    tiles = lax.all_to_all(
        partial_tiles.reshape(pair_count, share_rows, share_cols), "pair", 0, 0, tiled=True
    )
    return outputs(tiles, occ_energy, virt_energy)


def solution(mesh):
    in_specs = (P("pair", "aux"), P("aux", "pair"), P(), P())
    out_specs = (P("pair", "aux"), P())
    stacked = mesh.shape["aux"] == 2 and mesh.shape["pair"] == LAYERS * PLANE
    return jax.shard_map(
        shards_stacked if stacked else shards_any,
        mesh=mesh,
        in_specs=in_specs,
        out_specs=out_specs,
        check_vma=False,
    )
```

```python
import functools

import jax
import jax.numpy as jnp
from jax import lax
from jax.experimental import pallas as pl
from jax.experimental.pallas import tpu as pltpu
from jax.sharding import PartitionSpec as P

AXES = ("aux", "pair")
LAYERS = 4
PLANE = 4
TURN = (1, 2)


def total_of(value, axes):
    count = lax.axis_size(axes)
    sent = jnp.broadcast_to(value, (count, 8, 128))
    return jnp.sum(lax.all_to_all(sent, axes, 0, 0, tiled=True)[:, 0, 0])


def nt_dot(left, right):
    return lax.dot_general(
        left, right, (((1,), (1,)), ((), ())), preferred_element_type=jnp.float32
    )


def outputs(tiles, occ_energy, virt_energy):
    pair_count, share_rows, share_cols = tiles.shape
    aux_id = lax.axis_index("aux")
    pair_id = lax.axis_index("pair")
    integrals = jnp.sum(tiles.astype(jnp.float32), axis=0)
    pair_gap = (virt_energy[None, :] - occ_energy[:, None]).reshape(-1)
    row_gap = lax.dynamic_slice_in_dim(pair_gap, pair_id * share_rows, share_rows, 0)
    col_gap = lax.dynamic_slice_in_dim(pair_gap, aux_id * share_cols, share_cols, 0)
    denominator = row_gap[:, None] + col_gap[None, :]
    amplitudes = integrals / denominator
    energy = -total_of(jnp.sum(integrals * amplitudes), AXES)
    return (amplitudes, energy)


def shards_any(metric_factor, three_centre, occ_energy, virt_energy):
    aux_count = lax.axis_size("aux")
    pair_count = lax.axis_size("pair")
    pairs_total = three_centre.shape[1] * pair_count
    share_cols = pairs_total // aux_count
    share_rows = pairs_total // pair_count
    partial_fit = jnp.dot(
        metric_factor,
        lax.all_gather(three_centre, "pair", axis=1, tiled=True),
        preferred_element_type=jnp.float32,
    )
    own_share = lax.psum_scatter(partial_fit, "aux", scatter_dimension=1, tiled=True).astype(
        jnp.bfloat16
    )
    fitted = lax.all_gather(own_share, "aux", axis=1, tiled=True)
    partial_tiles = lax.dot_general(
        fitted, own_share, (((0,), (0,)), ((), ())), preferred_element_type=jnp.float32
    ).astype(jnp.bfloat16)
    tiles = lax.all_to_all(partial_tiles, "pair", 0, 0, tiled=True)
    return outputs(tiles.reshape(pair_count, share_rows, share_cols), occ_energy, virt_energy)


def layers_of(core):
    return range(0, LAYERS) if core == 0 else range(LAYERS // 2, LAYERS)


def along(turn):
    pairs = []
    for core in range(2):
        for z in layers_of(core):
            at = (core * LAYERS + z) * PLANE
            pairs += [(at + i, at + (i ^ turn[core])) for i in range(PLANE)]
    return pairs


def climbs(stage):
    steps = [[(z, (z + 1) % LAYERS) for z in range(LAYERS)]]
    steps.append([(z, z + 1) for z in range(stage - 1, LAYERS - 1)])
    if stage == LAYERS - 1:
        steps[1].append((LAYERS - 1, LAYERS - 2))
    pairs = []
    for core in range(2):
        for source, target in steps[core]:
            at, to = [(core * LAYERS + z) * PLANE for z in (source, target)]
            pairs += [(at + i, to + i) for i in range(PLANE)]
    return pairs


def tied(value, after):
    return lax.optimization_barrier((value, *after))[0] if after else value


def fit_kernel(flags, own, near, far, both, factor, *rest):
    *before, out = rest
    wide = own.shape[0]
    turned = flags[1] * wide
    places = [
        0,
        pl.multiple_of(2 * wide - turned, 32),
        pl.multiple_of(wide + turned, 32),
        3 * wide,
    ]

    @pl.when(flags[0] == 1)
    def _():
        total = lax.dot_general(
            jnp.concatenate([own[...], near[...], far[...], both[...]]),
            factor[...],
            (((1,), (1,)), ((), ())),
            preferred_element_type=jnp.float32,
        )
        for i, at in enumerate(places):
            part = total[i * wide : (i + 1) * wide]
            if before:
                part += before[0][pl.ds(at, wide), :]
            out[pl.ds(at, wide), :] = part.astype(out.dtype)

    @pl.when(flags[0] == 0)
    def _():
        out[...] = jnp.zeros(out.shape, out.dtype)


def fit(flags, pieces, factor, part=0, parts=1, before=None, dtype=jnp.bfloat16):
    depth = factor.shape[1] // parts
    wide = sum(piece.shape[0] for piece in pieces)
    rows = factor.shape[0]
    step = min(rows, 256)
    whole = pl.BlockSpec((pieces[0].shape[0], depth), lambda i, flags: (0, part))
    alone = pl.BlockSpec((pieces[0].shape[0], depth), lambda i, flags: (0, 0))
    tile = pl.BlockSpec((wide, step), lambda i, flags: (0, i))
    return pl.pallas_call(
        fit_kernel,
        out_shape=jax.ShapeDtypeStruct((wide, rows), dtype),
        grid_spec=pltpu.PrefetchScalarGridSpec(
            num_scalar_prefetch=1,
            grid=(rows // step,),
            in_specs=[alone if piece.shape[1] == depth else whole for piece in pieces]
            + [pl.BlockSpec((step, depth), lambda i, flags: (i * flags[0], part))]
            + ([] if before is None else [tile]),
            out_specs=tile,
        ),
        compiler_params=pltpu.CompilerParams(vmem_limit_bytes=40 << 20),
        cost_estimate=pl.CostEstimate(
            flops=2 * wide * depth * rows,
            bytes_accessed=2 * (depth * (wide + rows) + wide * rows),
            transcendentals=0,
        ),
    )(flags, *pieces, factor, *(() if before is None else (before,)))


def shards_stacked(metric_factor, three_centre, occ_energy, virt_energy):
    aux_id = lax.axis_index("aux")
    pair_id = lax.axis_index("pair")
    layer = pair_id // PLANE
    place = pair_id % PLANE
    share_rows = three_centre.shape[1]
    pair_count = LAYERS * PLANE
    pairs_total = share_rows * pair_count
    share_cols = pairs_total // 2
    rows = metric_factor.shape[0]
    own = three_centre.T
    needed = jnp.logical_or(aux_id == 0, layer >= LAYERS // 2)
    crossed = []

    def cross(piece, turn, after=()):
        after = [*crossed[-4:][: max(len(crossed) - 3, 0)][:1], *after]
        crossed.append(lax.ppermute(tied(piece, after), AXES, along(turn)))
        return crossed[-1]

    def spread(piece, after=(), near=None, tie=()):
        near = tied(cross(piece, TURN), tie) if near is None else near
        far = cross(piece, TURN[::-1])
        return [piece, near, far, cross(near, TURN[::-1], after)]

    def climb(piece, stage, after=()):
        return lax.ppermute(tied(piece, after), AXES, climbs(stage))

    flags = jnp.stack([needed, aux_id == 0]).astype(jnp.int32)

    def fitted_of(pieces, *more):
        partial = fit(flags, pieces, metric_factor, *more)
        other = lax.ppermute(partial, "aux", [(0, 1), (1, 0)])
        total = partial.astype(jnp.float32) + other.astype(jnp.float32)
        return partial, total.astype(jnp.bfloat16)

    above_1 = climb(own, 1)
    plane_0 = spread(own)
    above_2 = climb(above_1, 2, plane_0[1:3])
    plane_1 = spread(above_1)
    turning = jnp.logical_and(aux_id == 1, layer == LAYERS - 1)
    above_3 = climb(jnp.where(turning, own, above_2), 3, plane_1[1:2])
    partial_0, fitted_0 = fitted_of(plane_0)
    plane_2 = spread(above_2, tie=[partial_0])
    partial_1, fitted_1 = fitted_of(plane_1)
    near_3 = climb(jnp.where(turning, plane_0[1], plane_2[1]), 3)
    half = own.shape[1] // 2
    far_3 = [cross(above_3[:, :half], TURN[::-1])]
    partial_2, fitted_2 = fitted_of(plane_2)
    near_3 = tied(near_3, [partial_1, plane_2[3]])
    far_3.append(climb(jnp.where(turning, plane_0[2], plane_2[2])[:, half:], 3, [near_3]))
    both_3 = [cross(near_3[:, i * half : (i + 1) * half], TURN[::-1]) for i in range(2)]
    both_3[0] = tied(both_3[0], [partial_2])
    partial_3 = fit(
        flags, [above_3, near_3, far_3[0], both_3[0]], metric_factor, 0, 2, None, jnp.float32
    )
    both_3[1] = tied(both_3[1], [partial_3])
    fitted_3 = fitted_of([above_3, near_3, far_3[1], both_3[1]], 1, 2, partial_3)[1]
    fitted = jnp.concatenate([fitted_0, fitted_1, fitted_2, fitted_3])
    blocks = fitted.reshape(pair_count, share_rows, rows)
    ordered = []
    for z in range(LAYERS):
        slot = (layer - z) % LAYERS
        for where in range(PLANE):
            offset = place ^ where
            at = slot * PLANE + offset
            ordered.append(lax.dynamic_index_in_dim(blocks, at, 0, keepdims=False))
    fitted = jnp.concatenate(ordered)
    own_share = lax.dynamic_slice_in_dim(fitted, aux_id * share_cols, share_cols, 0)
    grid = (LAYERS, PLANE, share_rows, rows)
    turned = jnp.swapaxes(fitted.reshape(grid), 0, 1).reshape(fitted.shape)
    partial_tiles = nt_dot(turned, own_share).astype(jnp.bfloat16)
    tiles = partial_tiles.reshape(PLANE, LAYERS, share_rows, share_cols)
    chips = [list(range(z * PLANE, (z + 1) * PLANE)) for z in range(LAYERS)]
    for groups in (chips, [list(group) for group in zip(*chips)]):
        tiles = lax.all_to_all(tiles, "pair", 0, 0, tiled=True, axis_index_groups=groups)
        if groups is chips:
            tiles = jnp.sum(tiles.astype(jnp.float32), axis=0).astype(jnp.bfloat16)
    return outputs(tiles, occ_energy, virt_energy)


def solution(mesh):
    in_specs = (P("pair", "aux"), P("aux", "pair"), P(), P())
    out_specs = (P("pair", "aux"), P())
    stacked = mesh.shape["aux"] == 2 and mesh.shape["pair"] == LAYERS * PLANE
    return jax.shard_map(
        shards_stacked if stacked else shards_any,
        mesh=mesh,
        in_specs=in_specs,
        out_specs=out_specs,
        check_vma=False,
    )
```

```python
import functools

import jax
import jax.numpy as jnp
from jax import lax
from jax.experimental import pallas as pl
from jax.experimental.pallas import tpu as pltpu
from jax.sharding import PartitionSpec as P

AXES = ("aux", "pair")
LAYERS = 4
PLANE = 4
TURN = (1, 2)


def total_of(value, axes):
    count = lax.axis_size(axes)
    sent = jnp.broadcast_to(value, (count, 8, 128))
    return jnp.sum(lax.all_to_all(sent, axes, 0, 0, tiled=True)[:, 0, 0])


def nt_dot(left, right):
    return lax.dot_general(
        left, right, (((1,), (1,)), ((), ())), preferred_element_type=jnp.float32
    )


def outputs(tiles, occ_energy, virt_energy):
    pair_count, share_rows, share_cols = tiles.shape
    aux_id = lax.axis_index("aux")
    pair_id = lax.axis_index("pair")
    integrals = jnp.sum(tiles.astype(jnp.float32), axis=0)
    pair_gap = (virt_energy[None, :] - occ_energy[:, None]).reshape(-1)
    row_gap = lax.dynamic_slice_in_dim(pair_gap, pair_id * share_rows, share_rows, 0)
    col_gap = lax.dynamic_slice_in_dim(pair_gap, aux_id * share_cols, share_cols, 0)
    denominator = row_gap[:, None] + col_gap[None, :]
    amplitudes = integrals / denominator
    energy = -total_of(jnp.sum(integrals * amplitudes), AXES)
    return (amplitudes, energy)


def shards_any(metric_factor, three_centre, occ_energy, virt_energy):
    aux_count = lax.axis_size("aux")
    pair_count = lax.axis_size("pair")
    pairs_total = three_centre.shape[1] * pair_count
    share_cols = pairs_total // aux_count
    share_rows = pairs_total // pair_count
    partial_fit = jnp.dot(
        metric_factor,
        lax.all_gather(three_centre, "pair", axis=1, tiled=True),
        preferred_element_type=jnp.float32,
    )
    own_share = lax.psum_scatter(partial_fit, "aux", scatter_dimension=1, tiled=True).astype(
        jnp.bfloat16
    )
    fitted = lax.all_gather(own_share, "aux", axis=1, tiled=True)
    partial_tiles = lax.dot_general(
        fitted, own_share, (((0,), (0,)), ((), ())), preferred_element_type=jnp.float32
    ).astype(jnp.bfloat16)
    tiles = lax.all_to_all(partial_tiles, "pair", 0, 0, tiled=True)
    return outputs(tiles.reshape(pair_count, share_rows, share_cols), occ_energy, virt_energy)


def layers_of(core):
    return range(0, LAYERS) if core == 0 else range(LAYERS // 2, LAYERS)


def along(turn):
    pairs = []
    for core in range(2):
        for z in layers_of(core):
            at = (core * LAYERS + z) * PLANE
            pairs += [(at + i, at + (i ^ turn[core])) for i in range(PLANE)]
    return pairs


def climbs(stage):
    steps = [[(z, (z + 1) % LAYERS) for z in range(LAYERS)]]
    steps.append([(z, z + 1) for z in range(stage - 1, LAYERS - 1)])
    if stage == LAYERS - 1:
        steps[1].append((LAYERS - 1, LAYERS - 2))
    pairs = []
    for core in range(2):
        for source, target in steps[core]:
            at, to = [(core * LAYERS + z) * PLANE for z in (source, target)]
            pairs += [(at + i, to + i) for i in range(PLANE)]
    return pairs


def tied(value, after):
    return lax.optimization_barrier((value, *after))[0] if after else value


def fit_kernel(count, flags, *refs):
    pieces, factor = refs[:count], refs[count]
    *before, out = refs[count + 1 :]
    wide = pieces[0].shape[0]
    places = [i * wide for i in range(count)]
    turned = flags[1] * wide
    lead = max(count - PLANE, 0) * wide
    places[1 + lead // wide] = pl.multiple_of(lead + 2 * wide - turned, 32)
    places[2 + lead // wide] = pl.multiple_of(lead + wide + turned, 32)

    @pl.when(flags[0] == 1)
    def _():
        total = lax.dot_general(
            jnp.concatenate([piece[...] for piece in pieces]),
            factor[...],
            (((1,), (1,)), ((), ())),
            preferred_element_type=jnp.float32,
        )
        for i, at in enumerate(places):
            part = total[i * wide : (i + 1) * wide]
            if before:
                part += before[0][pl.ds(at, wide), :]
            out[pl.ds(at, wide), :] = part.astype(out.dtype)

    @pl.when(flags[0] == 0)
    def _():
        out[...] = jnp.zeros(out.shape, out.dtype)


def fit(flags, pieces, factor, part=0, parts=1, before=None, dtype=jnp.bfloat16):
    depth = factor.shape[1] // parts
    wide = sum(piece.shape[0] for piece in pieces)
    rows = factor.shape[0]
    step = min(rows, 256)
    whole = pl.BlockSpec((pieces[0].shape[0], depth), lambda i, flags: (0, part))
    alone = pl.BlockSpec((pieces[0].shape[0], depth), lambda i, flags: (0, 0))
    tile = pl.BlockSpec((wide, step), lambda i, flags: (0, i))
    return pl.pallas_call(
        functools.partial(fit_kernel, len(pieces)),
        out_shape=jax.ShapeDtypeStruct((wide, rows), dtype),
        grid_spec=pltpu.PrefetchScalarGridSpec(
            num_scalar_prefetch=1,
            grid=(rows // step,),
            in_specs=[alone if piece.shape[1] == depth else whole for piece in pieces]
            + [pl.BlockSpec((step, depth), lambda i, flags: (i * flags[0], part))]
            + ([] if before is None else [tile]),
            out_specs=tile,
        ),
        compiler_params=pltpu.CompilerParams(vmem_limit_bytes=40 << 20),
        cost_estimate=pl.CostEstimate(
            flops=2 * wide * depth * rows,
            bytes_accessed=2 * (depth * (wide + rows) + wide * rows),
            transcendentals=0,
        ),
    )(flags, *pieces, factor, *(() if before is None else (before,)))


def shards_stacked(metric_factor, three_centre, occ_energy, virt_energy):
    aux_id = lax.axis_index("aux")
    pair_id = lax.axis_index("pair")
    layer = pair_id // PLANE
    place = pair_id % PLANE
    share_rows = three_centre.shape[1]
    pair_count = LAYERS * PLANE
    pairs_total = share_rows * pair_count
    share_cols = pairs_total // 2
    rows = metric_factor.shape[0]
    own = three_centre.T
    needed = jnp.logical_or(aux_id == 0, layer >= LAYERS // 2)
    crossed = []

    def cross(piece, turn, after=()):
        after = [*crossed[-4:][: max(len(crossed) - 3, 0)][:1], *after]
        crossed.append(lax.ppermute(tied(piece, after), AXES, along(turn)))
        return crossed[-1]

    def spread(piece, after=(), near=None, tie=()):
        near = tied(cross(piece, TURN), tie) if near is None else near
        far = cross(piece, TURN[::-1])
        return [piece, near, far, cross(near, TURN[::-1], after)]

    def climb(piece, stage, after=()):
        return lax.ppermute(tied(piece, after), AXES, climbs(stage))

    flags = jnp.stack([needed, aux_id == 0]).astype(jnp.int32)

    def fitted_of(pieces, *more):
        partial = fit(flags, pieces, metric_factor, *more)
        other = lax.ppermute(partial, "aux", [(0, 1), (1, 0)])
        total = partial.astype(jnp.float32) + other.astype(jnp.float32)
        return partial, total.astype(jnp.bfloat16)

    above_1 = climb(own, 1)
    plane_0 = spread(own)
    above_2 = climb(above_1, 2, plane_0[1:3])
    plane_1 = spread(above_1)
    turning = jnp.logical_and(aux_id == 1, layer == LAYERS - 1)
    above_3 = climb(jnp.where(turning, own, above_2), 3, plane_1[1:2])
    partial_0, fitted_0 = fitted_of(plane_0)
    plane_2 = spread(above_2, tie=[partial_0])
    partial_1, fitted_1 = fitted_of(plane_1)
    near_3 = climb(jnp.where(turning, plane_0[1], plane_2[1]), 3)
    half = own.shape[1] // 2
    far_3 = [cross(above_3[:, :half], TURN[::-1])]
    partial_2, fitted_2 = fitted_of(plane_2[:3])
    near_3 = tied(near_3, [partial_1, partial_2, plane_2[3]])
    far_3.append(climb(jnp.where(turning, plane_0[2], plane_2[2])[:, half:], 3, [near_3]))
    both_3 = [cross(near_3[:, i * half : (i + 1) * half], TURN[::-1]) for i in range(2)]
    both_3[0] = tied(both_3[0], [fitted_0, fitted_1, fitted_2])
    partial_3 = fit(
        flags, [plane_2[3], above_3, near_3, far_3[0], both_3[0]], metric_factor, 0, 2, None, jnp.float32
    )
    both_3[1] = tied(both_3[1], [partial_3])
    fitted_3 = fitted_of([plane_2[3], above_3, near_3, far_3[1], both_3[1]], 1, 2, partial_3)[1]
    fitted = jnp.concatenate([fitted_0, fitted_1, fitted_2, fitted_3])
    blocks = fitted.reshape(pair_count, share_rows, rows)
    ordered = []
    for z in range(LAYERS):
        slot = (layer - z) % LAYERS
        for where in range(PLANE):
            offset = place ^ where
            at = slot * PLANE + offset
            ordered.append(lax.dynamic_index_in_dim(blocks, at, 0, keepdims=False))
    fitted = jnp.concatenate(ordered)
    own_share = lax.dynamic_slice_in_dim(fitted, aux_id * share_cols, share_cols, 0)
    grid = (LAYERS, PLANE, share_rows, rows)
    turned = jnp.swapaxes(fitted.reshape(grid), 0, 1).reshape(fitted.shape)
    partial_tiles = nt_dot(turned, own_share).astype(jnp.bfloat16)
    tiles = partial_tiles.reshape(PLANE, LAYERS, share_rows, share_cols)
    chips = [list(range(z * PLANE, (z + 1) * PLANE)) for z in range(LAYERS)]
    for groups in (chips, [list(group) for group in zip(*chips)]):
        tiles = lax.all_to_all(tiles, "pair", 0, 0, tiled=True, axis_index_groups=groups)
        if groups is chips:
            tiles = jnp.sum(tiles.astype(jnp.float32), axis=0).astype(jnp.bfloat16)
    return outputs(tiles, occ_energy, virt_energy)


def solution(mesh):
    in_specs = (P("pair", "aux"), P("aux", "pair"), P(), P())
    out_specs = (P("pair", "aux"), P())
    stacked = mesh.shape["aux"] == 2 and mesh.shape["pair"] == LAYERS * PLANE
    return jax.shard_map(
        shards_stacked if stacked else shards_any,
        mesh=mesh,
        in_specs=in_specs,
        out_specs=out_specs,
        check_vma=False,
    )
```

```python
import functools

import jax
import jax.numpy as jnp
from jax import lax
from jax.experimental import pallas as pl
from jax.experimental.pallas import tpu as pltpu
from jax.sharding import PartitionSpec as P

AXES = ("aux", "pair")
LAYERS = 4
PLANE = 4
TURN = (1, 2)


def total_of(value, axes):
    count = lax.axis_size(axes)
    sent = jnp.broadcast_to(value, (count, 1, 128))
    return jnp.sum(lax.all_to_all(sent, axes, 0, 0, tiled=True)[:, 0, 0])


def nt_dot(left, right):
    return lax.dot_general(
        left, right, (((1,), (1,)), ((), ())), preferred_element_type=jnp.float32
    )


def outputs(tiles, occ_energy, virt_energy):
    pair_count, share_rows, share_cols = tiles.shape
    aux_id = lax.axis_index("aux")
    pair_id = lax.axis_index("pair")
    integrals = jnp.sum(tiles.astype(jnp.float32), axis=0)
    pair_gap = (virt_energy[None, :] - occ_energy[:, None]).reshape(-1)
    row_gap = lax.dynamic_slice_in_dim(pair_gap, pair_id * share_rows, share_rows, 0)
    col_gap = lax.dynamic_slice_in_dim(pair_gap, aux_id * share_cols, share_cols, 0)
    denominator = row_gap[:, None] + col_gap[None, :]
    amplitudes = integrals / denominator
    energy = -total_of(jnp.sum(integrals * amplitudes), AXES)
    return (amplitudes, energy)


def shards_any(metric_factor, three_centre, occ_energy, virt_energy):
    aux_count = lax.axis_size("aux")
    pair_count = lax.axis_size("pair")
    pairs_total = three_centre.shape[1] * pair_count
    share_cols = pairs_total // aux_count
    share_rows = pairs_total // pair_count
    partial_fit = jnp.dot(
        metric_factor,
        lax.all_gather(three_centre, "pair", axis=1, tiled=True),
        preferred_element_type=jnp.float32,
    )
    own_share = lax.psum_scatter(partial_fit, "aux", scatter_dimension=1, tiled=True).astype(
        jnp.bfloat16
    )
    fitted = lax.all_gather(own_share, "aux", axis=1, tiled=True)
    partial_tiles = lax.dot_general(
        fitted, own_share, (((0,), (0,)), ((), ())), preferred_element_type=jnp.float32
    ).astype(jnp.bfloat16)
    tiles = lax.all_to_all(partial_tiles, "pair", 0, 0, tiled=True)
    return outputs(tiles.reshape(pair_count, share_rows, share_cols), occ_energy, virt_energy)


def layers_of(core):
    return range(0, LAYERS) if core == 0 else range(LAYERS // 2, LAYERS)


def along(turn):
    pairs = []
    for core in range(2):
        for z in layers_of(core):
            at = (core * LAYERS + z) * PLANE
            pairs += [(at + i, at + (i ^ turn[core])) for i in range(PLANE)]
    return pairs


def climbs(stage):
    steps = [[(z, (z + 1) % LAYERS) for z in range(LAYERS)]]
    steps.append([(z, z + 1) for z in range(stage - 1, LAYERS - 1)])
    if stage == LAYERS - 1:
        steps[1].append((LAYERS - 1, LAYERS - 2))
    pairs = []
    for core in range(2):
        for source, target in steps[core]:
            at, to = [(core * LAYERS + z) * PLANE for z in (source, target)]
            pairs += [(at + i, to + i) for i in range(PLANE)]
    return pairs


def tied(value, after):
    return lax.optimization_barrier((value, *after))[0] if after else value


def fit_kernel(count, flags, *refs):
    pieces, factor = refs[:count], refs[count]
    *before, out = refs[count + 1 :]
    wide = pieces[0].shape[0]
    places = [i * wide for i in range(count)]
    turned = flags[1] * wide
    lead = max(count - PLANE, 0) * wide
    places[1 + lead // wide] = pl.multiple_of(lead + 2 * wide - turned, 32)
    places[2 + lead // wide] = pl.multiple_of(lead + wide + turned, 32)

    @pl.when(flags[0] == 1)
    def _():
        total = lax.dot_general(
            jnp.concatenate([piece[...] for piece in pieces]),
            factor[...],
            (((1,), (1,)), ((), ())),
            preferred_element_type=jnp.float32,
        )
        for i, at in enumerate(places):
            part = total[i * wide : (i + 1) * wide]
            if before:
                part += before[0][pl.ds(at, wide), :]
            out[pl.ds(at, wide), :] = part.astype(out.dtype)

    @pl.when(flags[0] == 0)
    def _():
        out[...] = jnp.zeros(out.shape, out.dtype)


def fit(flags, pieces, factor, part=0, parts=1, before=None, dtype=jnp.bfloat16):
    depth = factor.shape[1] // parts
    wide = sum(piece.shape[0] for piece in pieces)
    rows = factor.shape[0]
    step = min(rows, 256)
    whole = pl.BlockSpec((pieces[0].shape[0], depth), lambda i, flags: (0, part))
    alone = pl.BlockSpec((pieces[0].shape[0], depth), lambda i, flags: (0, 0))
    tile = pl.BlockSpec((wide, step), lambda i, flags: (0, i))
    return pl.pallas_call(
        functools.partial(fit_kernel, len(pieces)),
        out_shape=jax.ShapeDtypeStruct((wide, rows), dtype),
        grid_spec=pltpu.PrefetchScalarGridSpec(
            num_scalar_prefetch=1,
            grid=(rows // step,),
            in_specs=[alone if piece.shape[1] == depth else whole for piece in pieces]
            + [pl.BlockSpec((step, depth), lambda i, flags: (i * flags[0], part))]
            + ([] if before is None else [tile]),
            out_specs=tile,
        ),
        compiler_params=pltpu.CompilerParams(vmem_limit_bytes=40 << 20),
        cost_estimate=pl.CostEstimate(
            flops=2 * wide * depth * rows,
            bytes_accessed=2 * (depth * (wide + rows) + wide * rows),
            transcendentals=0,
        ),
    )(flags, *pieces, factor, *(() if before is None else (before,)))


def shards_stacked(metric_factor, three_centre, occ_energy, virt_energy):
    aux_id = lax.axis_index("aux")
    pair_id = lax.axis_index("pair")
    layer = pair_id // PLANE
    place = pair_id % PLANE
    share_rows = three_centre.shape[1]
    pair_count = LAYERS * PLANE
    pairs_total = share_rows * pair_count
    share_cols = pairs_total // 2
    rows = metric_factor.shape[0]
    own = three_centre.T
    needed = jnp.logical_or(aux_id == 0, layer >= LAYERS // 2)
    crossed = []

    def cross(piece, turn, after=()):
        after = [*crossed[-4:][: max(len(crossed) - 3, 0)][:1], *after]
        crossed.append(lax.ppermute(tied(piece, after), AXES, along(turn)))
        return crossed[-1]

    def spread(piece, after=(), near=None, tie=()):
        near = tied(cross(piece, TURN), tie) if near is None else near
        far = cross(piece, TURN[::-1])
        return [piece, near, far, cross(near, TURN[::-1], after)]

    def climb(piece, stage, after=()):
        return lax.ppermute(tied(piece, after), AXES, climbs(stage))

    flags = jnp.stack([needed, aux_id == 0]).astype(jnp.int32)

    def fitted_of(pieces, *more):
        partial = fit(flags, pieces, metric_factor, *more)
        other = lax.ppermute(partial, "aux", [(0, 1), (1, 0)])
        total = partial.astype(jnp.float32) + other.astype(jnp.float32)
        return partial, total.astype(jnp.bfloat16)

    above_1 = climb(own, 1)
    plane_0 = spread(own)
    above_2 = climb(above_1, 2, plane_0[1:3])
    plane_1 = spread(above_1)
    turning = jnp.logical_and(aux_id == 1, layer == LAYERS - 1)
    above_3 = climb(jnp.where(turning, own, above_2), 3, plane_1[1:2])
    partial_0, fitted_0 = fitted_of(plane_0)
    plane_2 = spread(above_2, tie=[partial_0])
    partial_1, fitted_1 = fitted_of(plane_1)
    near_3 = climb(jnp.where(turning, plane_0[1], plane_2[1]), 3)
    half = own.shape[1] // 2
    far_3 = [cross(above_3[:, :half], TURN[::-1])]
    partial_2, fitted_2 = fitted_of(plane_2[:3])
    near_3 = tied(near_3, [partial_1, partial_2, plane_2[3]])
    far_3.append(climb(jnp.where(turning, plane_0[2], plane_2[2])[:, half:], 3, [near_3]))
    both_3 = [cross(near_3[:, i * half : (i + 1) * half], TURN[::-1]) for i in range(2)]
    both_3[0] = tied(both_3[0], [fitted_0, fitted_1, fitted_2])
    partial_3 = fit(
        flags, [plane_2[3], above_3, near_3, far_3[0], both_3[0]], metric_factor, 0, 2, None, jnp.float32
    )
    both_3[1] = tied(both_3[1], [partial_3])
    fitted_3 = fitted_of([plane_2[3], above_3, near_3, far_3[1], both_3[1]], 1, 2, partial_3)[1]
    fitted = jnp.concatenate([fitted_0, fitted_1, fitted_2, fitted_3])
    blocks = fitted.reshape(pair_count, share_rows, rows)
    ordered = []
    for z in range(LAYERS):
        slot = (layer - z) % LAYERS
        for where in range(PLANE):
            offset = place ^ where
            at = slot * PLANE + offset
            ordered.append(lax.dynamic_index_in_dim(blocks, at, 0, keepdims=False))
    fitted = jnp.concatenate(ordered)
    own_share = lax.dynamic_slice_in_dim(fitted, aux_id * share_cols, share_cols, 0)
    grid = (LAYERS, PLANE, share_rows, rows)
    turned = jnp.swapaxes(fitted.reshape(grid), 0, 1).reshape(fitted.shape)
    partial_tiles = nt_dot(turned, own_share).astype(jnp.bfloat16)
    tiles = partial_tiles.reshape(PLANE, LAYERS, share_rows, share_cols)
    chips = [list(range(z * PLANE, (z + 1) * PLANE)) for z in range(LAYERS)]
    tiles = lax.all_to_all(tiles, "pair", 0, 0, tiled=True, axis_index_groups=chips)
    sums = jnp.sum(tiles.astype(jnp.float32), axis=0)
    columns = [list(group) for group in zip(*chips)]
    tiles = lax.all_to_all(
        sums.astype(jnp.bfloat16), "pair", 0, 0, tiled=True, axis_index_groups=columns
    )
    own_sum = lax.dynamic_index_in_dim(sums, layer, 0, keepdims=False)
    is_own = (jnp.arange(LAYERS) == layer)[:, None, None]
    tiles = jnp.where(is_own, own_sum[None], tiles.astype(jnp.float32))
    return outputs(tiles, occ_energy, virt_energy)


def solution(mesh):
    in_specs = (P("pair", "aux"), P("aux", "pair"), P(), P())
    out_specs = (P("pair", "aux"), P())
    stacked = mesh.shape["aux"] == 2 and mesh.shape["pair"] == LAYERS * PLANE
    return jax.shard_map(
        shards_stacked if stacked else shards_any,
        mesh=mesh,
        in_specs=in_specs,
        out_specs=out_specs,
        check_vma=False,
    )
```

```python
import functools

import jax
import jax.numpy as jnp
from jax import lax
from jax.experimental import pallas as pl
from jax.experimental.pallas import tpu as pltpu
from jax.sharding import PartitionSpec as P

AXES = ("aux", "pair")
LAYERS = 4
PLANE = 4
TURN = (1, 2)


def total_of(value, axes):
    count = lax.axis_size(axes)
    sent = jnp.broadcast_to(value, (count, 1, 128))
    return jnp.sum(lax.all_to_all(sent, axes, 0, 0, tiled=True)[:, 0, 0])


def nt_dot(left, right):
    return lax.dot_general(
        left, right, (((1,), (1,)), ((), ())), preferred_element_type=jnp.float32
    )


def outputs(tiles, occ_energy, virt_energy):
    pair_count, share_rows, share_cols = tiles.shape
    aux_id = lax.axis_index("aux")
    pair_id = lax.axis_index("pair")
    integrals = jnp.sum(tiles.astype(jnp.float32), axis=0)
    pair_gap = (virt_energy[None, :] - occ_energy[:, None]).reshape(-1)
    row_gap = lax.dynamic_slice_in_dim(pair_gap, pair_id * share_rows, share_rows, 0)
    col_gap = lax.dynamic_slice_in_dim(pair_gap, aux_id * share_cols, share_cols, 0)
    denominator = row_gap[:, None] + col_gap[None, :]
    amplitudes = integrals / denominator
    energy = -total_of(jnp.sum(integrals * amplitudes), AXES)
    return (amplitudes, energy)


def shards_any(metric_factor, three_centre, occ_energy, virt_energy):
    aux_count = lax.axis_size("aux")
    pair_count = lax.axis_size("pair")
    pairs_total = three_centre.shape[1] * pair_count
    share_cols = pairs_total // aux_count
    share_rows = pairs_total // pair_count
    partial_fit = jnp.dot(
        metric_factor,
        lax.all_gather(three_centre, "pair", axis=1, tiled=True),
        preferred_element_type=jnp.float32,
    )
    own_share = lax.psum_scatter(partial_fit, "aux", scatter_dimension=1, tiled=True).astype(
        jnp.bfloat16
    )
    fitted = lax.all_gather(own_share, "aux", axis=1, tiled=True)
    partial_tiles = lax.dot_general(
        fitted, own_share, (((0,), (0,)), ((), ())), preferred_element_type=jnp.float32
    ).astype(jnp.bfloat16)
    tiles = lax.all_to_all(partial_tiles, "pair", 0, 0, tiled=True)
    return outputs(tiles.reshape(pair_count, share_rows, share_cols), occ_energy, virt_energy)


def layers_of(core):
    return range(0, LAYERS) if core == 0 else range(LAYERS // 2, LAYERS)


def along(turn):
    pairs = []
    for core in range(2):
        for z in layers_of(core):
            at = (core * LAYERS + z) * PLANE
            pairs += [(at + i, at + (i ^ turn[core])) for i in range(PLANE)]
    return pairs


def climbs(stage):
    steps = [[(z, (z + 1) % LAYERS) for z in range(LAYERS)]]
    steps.append([(z, z + 1) for z in range(stage - 1, LAYERS - 1)])
    if stage == LAYERS - 1:
        steps[1].append((LAYERS - 1, LAYERS - 2))
    pairs = []
    for core in range(2):
        for source, target in steps[core]:
            at, to = [(core * LAYERS + z) * PLANE for z in (source, target)]
            pairs += [(at + i, to + i) for i in range(PLANE)]
    return pairs


def tied(value, after):
    return lax.optimization_barrier((value, *after))[0] if after else value


def fit_kernel(count, flags, *refs):
    pieces, factor = refs[:count], refs[count]
    *before, out = refs[count + 1 :]
    wide = pieces[0].shape[0]
    places = [i * wide for i in range(count)]
    turned = flags[1] * wide
    lead = max(count - PLANE, 0) * wide
    places[1 + lead // wide] = pl.multiple_of(lead + 2 * wide - turned, 32)
    places[2 + lead // wide] = pl.multiple_of(lead + wide + turned, 32)

    @pl.when(flags[0] == 1)
    def _():
        total = lax.dot_general(
            jnp.concatenate([piece[...] for piece in pieces]),
            factor[...],
            (((1,), (1,)), ((), ())),
            preferred_element_type=jnp.float32,
        )
        for i, at in enumerate(places):
            part = total[i * wide : (i + 1) * wide]
            if before:
                part += before[0][pl.ds(at, wide), :]
            out[pl.ds(at, wide), :] = part.astype(out.dtype)

    @pl.when(flags[0] == 0)
    def _():
        out[...] = jnp.zeros(out.shape, out.dtype)


def fit(flags, pieces, factor, part=0, parts=1, before=None, dtype=jnp.bfloat16):
    depth = factor.shape[1] // parts
    wide = sum(piece.shape[0] for piece in pieces)
    rows = factor.shape[0]
    step = min(rows, 256)
    whole = pl.BlockSpec((pieces[0].shape[0], depth), lambda i, flags: (0, part))
    alone = pl.BlockSpec((pieces[0].shape[0], depth), lambda i, flags: (0, 0))
    tile = pl.BlockSpec((wide, step), lambda i, flags: (0, i))
    return pl.pallas_call(
        functools.partial(fit_kernel, len(pieces)),
        out_shape=jax.ShapeDtypeStruct((wide, rows), dtype),
        grid_spec=pltpu.PrefetchScalarGridSpec(
            num_scalar_prefetch=1,
            grid=(rows // step,),
            in_specs=[alone if piece.shape[1] == depth else whole for piece in pieces]
            + [pl.BlockSpec((step, depth), lambda i, flags: (i * flags[0], part))]
            + ([] if before is None else [tile]),
            out_specs=tile,
        ),
        compiler_params=pltpu.CompilerParams(vmem_limit_bytes=40 << 20),
        cost_estimate=pl.CostEstimate(
            flops=2 * wide * depth * rows,
            bytes_accessed=2 * (depth * (wide + rows) + wide * rows),
            transcendentals=0,
        ),
    )(flags, *pieces, factor, *(() if before is None else (before,)))


def shards_stacked(metric_factor, three_centre, occ_energy, virt_energy):
    aux_id = lax.axis_index("aux")
    pair_id = lax.axis_index("pair")
    layer = pair_id // PLANE
    place = pair_id % PLANE
    share_rows = three_centre.shape[1]
    pair_count = LAYERS * PLANE
    pairs_total = share_rows * pair_count
    share_cols = pairs_total // 2
    rows = metric_factor.shape[0]
    own = three_centre.T
    needed = jnp.logical_or(aux_id == 0, layer >= LAYERS // 2)
    crossed = []

    def cross(piece, turn, after=()):
        after = [*crossed[-4:][: max(len(crossed) - 3, 0)][:1], *after]
        crossed.append(lax.ppermute(tied(piece, after), AXES, along(turn)))
        return crossed[-1]

    def spread(piece, after=(), near=None, tie=()):
        near = tied(cross(piece, TURN), tie) if near is None else near
        far = cross(piece, TURN[::-1])
        return [piece, near, far, cross(near, TURN[::-1], after)]

    def climb(piece, stage, after=()):
        return lax.ppermute(tied(piece, after), AXES, climbs(stage))

    flags = jnp.stack([needed, aux_id == 0]).astype(jnp.int32)

    def fitted_of(pieces, *more):
        partial = fit(flags, pieces, metric_factor, *more)
        other = lax.ppermute(partial, "aux", [(0, 1), (1, 0)])
        total = partial.astype(jnp.float32) + other.astype(jnp.float32)
        return partial, total.astype(jnp.bfloat16)

    above_1 = climb(own, 1)
    plane_0 = spread(own)
    above_2 = climb(above_1, 2, plane_0[1:3])
    plane_1 = spread(above_1)
    turning = jnp.logical_and(aux_id == 1, layer == LAYERS - 1)
    above_3 = climb(jnp.where(turning, own, above_2), 3, plane_1[1:2])
    partial_0, fitted_0 = fitted_of(plane_0)
    plane_2 = spread(above_2, tie=[partial_0])
    partial_1, fitted_1 = fitted_of(plane_1)
    near_3 = climb(jnp.where(turning, plane_0[1], plane_2[1]), 3)
    half = own.shape[1] // 2
    far_3 = [cross(above_3[:, :half], TURN[::-1])]
    partial_2, fitted_2 = fitted_of(plane_2[:3])
    near_3 = tied(near_3, [partial_1, partial_2, plane_2[3]])
    far_3.append(climb(jnp.where(turning, plane_0[2], plane_2[2])[:, half:], 3, [near_3]))
    both_3 = [cross(near_3[:, i * half : (i + 1) * half], TURN[::-1]) for i in range(2)]
    both_3[0] = tied(both_3[0], [fitted_0, fitted_1, fitted_2])
    partial_3 = fit(
        flags, [plane_2[3], above_3, near_3, far_3[0], both_3[0]], metric_factor, 0, 2, None, jnp.float32
    )
    both_3[1] = tied(both_3[1], [partial_3])
    fitted_3 = fitted_of([plane_2[3], above_3, near_3, far_3[1], both_3[1]], 1, 2, partial_3)[1]
    fitted = jnp.concatenate([fitted_0, fitted_1, fitted_2, fitted_3])
    blocks = fitted.reshape(pair_count, share_rows, rows)

    def block_of(z, offset):
        at = (layer - z) % LAYERS * PLANE + offset
        return lax.dynamic_index_in_dim(blocks, at, 0, keepdims=False)

    own_layers = LAYERS // 2
    own_share = jnp.concatenate(
        [
            block_of(aux_id * own_layers + z, place ^ where)
            for z in range(own_layers)
            for where in range(PLANE)
        ]
    )
    turn = [jnp.where(aux_id == 0, bits[0], bits[1]) for bits in (TURN, TURN[::-1])]

    def tiles_for(offsets):
        left = jnp.concatenate([block_of(z, offset) for offset in offsets for z in range(LAYERS)])
        return nt_dot(left, own_share).reshape(2, LAYERS, share_rows, share_cols)

    def everywhere(bits):
        count = LAYERS * PLANE
        return [(core * count + i, core * count + (i ^ bits[core])) for core in range(2) for i in range(count)]

    sent = tiles_for([turn[0], 3]).astype(jnp.bfloat16)
    came = lax.ppermute(sent, AXES, everywhere(TURN))
    kept = tiles_for([0, turn[1]]) + came.astype(jnp.float32)
    came = lax.ppermute(kept[1].astype(jnp.bfloat16), AXES, everywhere(TURN[::-1]))
    sums = kept[0] + came.astype(jnp.float32)
    chips = [list(range(z * PLANE, (z + 1) * PLANE)) for z in range(LAYERS)]
    columns = [list(group) for group in zip(*chips)]
    tiles = lax.all_to_all(
        sums.astype(jnp.bfloat16), "pair", 0, 0, tiled=True, axis_index_groups=columns
    )
    own_sum = lax.dynamic_index_in_dim(sums, layer, 0, keepdims=False)
    is_own = (jnp.arange(LAYERS) == layer)[:, None, None]
    tiles = jnp.where(is_own, own_sum[None], tiles.astype(jnp.float32))
    return outputs(tiles, occ_energy, virt_energy)


def solution(mesh):
    in_specs = (P("pair", "aux"), P("aux", "pair"), P(), P())
    out_specs = (P("pair", "aux"), P())
    stacked = mesh.shape["aux"] == 2 and mesh.shape["pair"] == LAYERS * PLANE
    return jax.shard_map(
        shards_stacked if stacked else shards_any,
        mesh=mesh,
        in_specs=in_specs,
        out_specs=out_specs,
        check_vma=False,
    )
```

```python
import functools

import jax
import jax.numpy as jnp
from jax import lax
from jax.experimental import pallas as pl
from jax.experimental.pallas import tpu as pltpu
from jax.sharding import PartitionSpec as P

AXES = ("aux", "pair")
LAYERS = 4
PLANE = 4
TURN = (1, 2)


def total_of(value, axes):
    count = lax.axis_size(axes)
    sent = jnp.broadcast_to(value, (count, 1, 128))
    return jnp.sum(lax.all_to_all(sent, axes, 0, 0, tiled=True)[:, 0, 0])


def nt_dot(left, right):
    return lax.dot_general(
        left, right, (((1,), (1,)), ((), ())), preferred_element_type=jnp.float32
    )


def outputs(tiles, occ_energy, virt_energy):
    pair_count, share_rows, share_cols = tiles.shape
    aux_id = lax.axis_index("aux")
    pair_id = lax.axis_index("pair")
    integrals = jnp.sum(tiles.astype(jnp.float32), axis=0)
    pair_gap = (virt_energy[None, :] - occ_energy[:, None]).reshape(-1)
    row_gap = lax.dynamic_slice_in_dim(pair_gap, pair_id * share_rows, share_rows, 0)
    col_gap = lax.dynamic_slice_in_dim(pair_gap, aux_id * share_cols, share_cols, 0)
    denominator = row_gap[:, None] + col_gap[None, :]
    amplitudes = integrals / denominator
    energy = -total_of(jnp.sum(integrals * amplitudes), AXES)
    return (amplitudes, energy)


def shards_any(metric_factor, three_centre, occ_energy, virt_energy):
    aux_count = lax.axis_size("aux")
    pair_count = lax.axis_size("pair")
    pairs_total = three_centre.shape[1] * pair_count
    share_cols = pairs_total // aux_count
    share_rows = pairs_total // pair_count
    partial_fit = jnp.dot(
        metric_factor,
        lax.all_gather(three_centre, "pair", axis=1, tiled=True),
        preferred_element_type=jnp.float32,
    )
    own_share = lax.psum_scatter(partial_fit, "aux", scatter_dimension=1, tiled=True).astype(
        jnp.bfloat16
    )
    fitted = lax.all_gather(own_share, "aux", axis=1, tiled=True)
    partial_tiles = lax.dot_general(
        fitted, own_share, (((0,), (0,)), ((), ())), preferred_element_type=jnp.float32
    ).astype(jnp.bfloat16)
    tiles = lax.all_to_all(partial_tiles, "pair", 0, 0, tiled=True)
    return outputs(tiles.reshape(pair_count, share_rows, share_cols), occ_energy, virt_energy)


def layers_of(core):
    return range(0, LAYERS) if core == 0 else range(LAYERS // 2, LAYERS)


def along(turn):
    pairs = []
    for core in range(2):
        for z in layers_of(core):
            at = (core * LAYERS + z) * PLANE
            pairs += [(at + i, at + (i ^ turn[core])) for i in range(PLANE)]
    return pairs


def climbs(stage):
    steps = [[(z, (z + 1) % LAYERS) for z in range(LAYERS)]]
    steps.append([(z, z + 1) for z in range(stage - 1, LAYERS - 1)])
    if stage == LAYERS - 1:
        steps[1].append((LAYERS - 1, LAYERS - 2))
    pairs = []
    for core in range(2):
        for source, target in steps[core]:
            at, to = [(core * LAYERS + z) * PLANE for z in (source, target)]
            pairs += [(at + i, to + i) for i in range(PLANE)]
    return pairs


def tied(value, after):
    return lax.optimization_barrier((value, *after))[0] if after else value


def fit_kernel(count, flags, *refs):
    pieces, factor = refs[:count], refs[count]
    *before, out = refs[count + 1 :]
    wide = pieces[0].shape[0]
    places = [i * wide for i in range(count)]
    turned = flags[1] * wide
    lead = max(count - PLANE, 0) * wide
    places[1 + lead // wide] = pl.multiple_of(lead + 2 * wide - turned, 32)
    places[2 + lead // wide] = pl.multiple_of(lead + wide + turned, 32)

    @pl.when(flags[0] == 1)
    def _():
        total = lax.dot_general(
            jnp.concatenate([piece[...] for piece in pieces]),
            factor[...],
            (((1,), (1,)), ((), ())),
            preferred_element_type=jnp.float32,
        )
        for i, at in enumerate(places):
            part = total[i * wide : (i + 1) * wide]
            if before:
                part += before[0][pl.ds(at, wide), :]
            out[pl.ds(at, wide), :] = part.astype(out.dtype)

    @pl.when(flags[0] == 0)
    def _():
        out[...] = jnp.zeros(out.shape, out.dtype)


def fit(flags, pieces, factor, part=0, parts=1, before=None, dtype=jnp.bfloat16):
    depth = factor.shape[1] // parts
    wide = sum(piece.shape[0] for piece in pieces)
    rows = factor.shape[0]
    step = min(rows, 256)
    whole = pl.BlockSpec((pieces[0].shape[0], depth), lambda i, flags: (0, part))
    alone = pl.BlockSpec((pieces[0].shape[0], depth), lambda i, flags: (0, 0))
    tile = pl.BlockSpec((wide, step), lambda i, flags: (0, i))
    return pl.pallas_call(
        functools.partial(fit_kernel, len(pieces)),
        out_shape=jax.ShapeDtypeStruct((wide, rows), dtype),
        grid_spec=pltpu.PrefetchScalarGridSpec(
            num_scalar_prefetch=1,
            grid=(rows // step,),
            in_specs=[alone if piece.shape[1] == depth else whole for piece in pieces]
            + [pl.BlockSpec((step, depth), lambda i, flags: (i * flags[0], part))]
            + ([] if before is None else [tile]),
            out_specs=tile,
        ),
        compiler_params=pltpu.CompilerParams(vmem_limit_bytes=40 << 20),
        cost_estimate=pl.CostEstimate(
            flops=2 * wide * depth * rows,
            bytes_accessed=2 * (depth * (wide + rows) + wide * rows),
            transcendentals=0,
        ),
    )(flags, *pieces, factor, *(() if before is None else (before,)))


def shards_stacked(metric_factor, three_centre, occ_energy, virt_energy):
    aux_id = lax.axis_index("aux")
    pair_id = lax.axis_index("pair")
    layer = pair_id // PLANE
    place = pair_id % PLANE
    share_rows = three_centre.shape[1]
    pair_count = LAYERS * PLANE
    pairs_total = share_rows * pair_count
    share_cols = pairs_total // 2
    rows = metric_factor.shape[0]
    own = three_centre.T
    needed = jnp.logical_or(aux_id == 0, layer >= LAYERS // 2)
    crossed = []

    def cross(piece, turn, after=()):
        after = [*crossed[-4:][: max(len(crossed) - 3, 0)][:1], *after]
        crossed.append(lax.ppermute(tied(piece, after), AXES, along(turn)))
        return crossed[-1]

    def spread(piece, after=(), near=None, tie=()):
        near = tied(cross(piece, TURN), tie) if near is None else near
        far = cross(piece, TURN[::-1])
        return [piece, near, far, cross(near, TURN[::-1], after)]

    def climb(piece, stage, after=()):
        return lax.ppermute(tied(piece, after), AXES, climbs(stage))

    flags = jnp.stack([needed, aux_id == 0]).astype(jnp.int32)

    def fitted_of(pieces, *more):
        partial = fit(flags, pieces, metric_factor, *more)
        other = lax.ppermute(partial, "aux", [(0, 1), (1, 0)])
        total = partial.astype(jnp.float32) + other.astype(jnp.float32)
        return partial, total.astype(jnp.bfloat16)

    above_1 = climb(own, 1)
    plane_0 = spread(own)
    above_2 = climb(above_1, 2, plane_0[1:3])
    plane_1 = spread(above_1)
    turning = jnp.logical_and(aux_id == 1, layer == LAYERS - 1)
    above_3 = climb(jnp.where(turning, own, above_2), 3, plane_1[1:2])
    partial_0, fitted_0 = fitted_of(plane_0)
    plane_2 = spread(above_2, tie=[partial_0])
    partial_1, fitted_1 = fitted_of(plane_1)
    near_3 = climb(jnp.where(turning, plane_0[1], plane_2[1]), 3)
    half = own.shape[1] // 2
    far_3 = [cross(above_3[:, :half], TURN[::-1])]
    partial_2, fitted_2 = fitted_of(plane_2[:3])
    near_3 = tied(near_3, [partial_1, partial_2, plane_2[3]])
    far_3.append(climb(jnp.where(turning, plane_0[2], plane_2[2])[:, half:], 3, [near_3]))
    both_3 = [cross(near_3[:, i * half : (i + 1) * half], TURN[::-1]) for i in range(2)]
    both_3[0] = tied(both_3[0], [fitted_0, fitted_1, fitted_2])
    partial_3 = fit(
        flags, [plane_2[3], above_3, near_3, far_3[0], both_3[0]], metric_factor, 0, 2, None, jnp.float32
    )
    both_3[1] = tied(both_3[1], [partial_3])
    fitted_3 = fitted_of([plane_2[3], above_3, near_3, far_3[1], both_3[1]], 1, 2, partial_3)[1]
    fitted = jnp.concatenate([fitted_0, fitted_1, fitted_2, fitted_3])
    blocks = fitted.reshape(pair_count, share_rows, rows)

    def block_of(z, offset):
        at = (layer - z) % LAYERS * PLANE + offset
        return lax.dynamic_index_in_dim(blocks, at, 0, keepdims=False)

    own_layers = LAYERS // 2
    own_share = jnp.concatenate(
        [
            block_of(aux_id * own_layers + z, place ^ where)
            for z in range(own_layers)
            for where in range(PLANE)
        ]
    )
    turn = [jnp.where(aux_id == 0, bits[0], bits[1]) for bits in (TURN, TURN[::-1])]

    def tiles_for(offsets):
        left = jnp.concatenate([block_of(z, offset) for offset in offsets for z in range(LAYERS)])
        return nt_dot(left, own_share).reshape(2, LAYERS, share_rows, share_cols)

    def everywhere(bits):
        count = LAYERS * PLANE
        return [(core * count + i, core * count + (i ^ bits[core])) for core in range(2) for i in range(count)]

    sent = tiles_for([turn[0], 3]).astype(jnp.bfloat16)
    came = lax.ppermute(sent, AXES, everywhere(TURN))
    kept = tiles_for([0, turn[1]]) + came.astype(jnp.float32)
    came = lax.ppermute(kept[1].astype(jnp.bfloat16), AXES, everywhere(TURN[::-1]))
    sums = kept[0] + came.astype(jnp.float32)
    terms = [lax.dynamic_index_in_dim(sums, layer, 0, keepdims=False)]
    for way in range(1, LAYERS):
        to = (layer + way) % LAYERS
        piece = lax.dynamic_index_in_dim(sums, to, 0, keepdims=False).astype(jnp.bfloat16)
        count = LAYERS * PLANE
        pairs = [
            (core * count + i, core * count + (i + way * PLANE) % count)
            for core in range(2)
            for i in range(count)
        ]
        terms.append(lax.ppermute(piece, AXES, pairs).astype(jnp.float32))
    tiles = jnp.stack(terms)
    return outputs(tiles, occ_energy, virt_energy)


def solution(mesh):
    in_specs = (P("pair", "aux"), P("aux", "pair"), P(), P())
    out_specs = (P("pair", "aux"), P())
    stacked = mesh.shape["aux"] == 2 and mesh.shape["pair"] == LAYERS * PLANE
    return jax.shard_map(
        shards_stacked if stacked else shards_any,
        mesh=mesh,
        in_specs=in_specs,
        out_specs=out_specs,
        check_vma=False,
    )
```
